32 devices in a mesh: groups: 2 (over x), ctx: 16 (over z, y, core).
Axes of the slice: x: 2, y: 2, z: 4, core: 2. Of those that a mesh axis runs over, the one named last changes fastest.
Arguments:
- queries: bfloat16 [8192, 1024], P(('groups', 'ctx')), parts along dimension 0, may hold values from -15 to 15
- key_rows: bfloat16 [8192, 1024], P(('groups', 'ctx')), parts along dimension 0, may hold values from -15 to 15
- value_rows: bfloat16 [8192, 1024], P(('groups', 'ctx')), parts along dimension 0, may hold values from -6 to 6
- out_grad: bfloat16 [8192, 2048], P(('groups', 'ctx')), parts along dimension 0, may hold values from -6 to 6
- out_weight: bfloat16 [2048, 1024], P('ctx'), may hold values from -0.1875 to 0.1875
- pair_allowed: int32 [64, 2], P('groups'), parts along dimension 0, may hold values 0 or 1
Outputs:
- layer_out: bfloat16 [8192, 2048], P(('groups', 'ctx')), parts along dimension 0
- query_grad: bfloat16 [8192, 1024], P(('groups', 'ctx')), parts along dimension 0
- key_grad: bfloat16 [8192, 1024], P(('groups', 'ctx')), parts along dimension 0
- value_grad: bfloat16 [8192, 1024], P(('groups', 'ctx')), parts along dimension 0
- weight_grad: float32 [4096, 1024], P(('groups', 'ctx')), parts along dimension 0
The draws below stay inside these ranges and needn't reach their ends.
There are 2 independent parts, one for each index of `groups`. The reference program is written for one: setup_inputs(seed, part) draws one part's arguments, and reference() takes and returns one part's arrays. A program takes and returns all parts, laid end to end along the dimension named above; an argument that names none is the same for every part. Nothing has to cross between parts.
All inputs are finite; a program needn't handle non-finite values.
Results may differ from the reference program's by a relative error of at most 0.011.
Values may be sent and summed in bfloat16 or wider, within the bound.
A program may use at most 128 MiB of HBM per device.

```python
import math
import jax
import jax.numpy as jnp
from jax import lax

D = 2048
H = 8
HD = 128
BLK = 128
SPAN = 2
BDEV = 2
NBLK = 32
TOKENS = 4096
N_CTX = 16


def draw_queries(key, part):
    drawn = jnp.clip(jax.random.normal(jax.random.fold_in(key, 7), (TOKENS, H * HD), jnp.float32), -4.0, 4.0)
    return drawn.astype(jnp.bfloat16)


def draw_key_rows(key, part):
    drawn = jnp.clip(jax.random.normal(jax.random.fold_in(key, 13), (TOKENS, H * HD), jnp.float32), -4.0, 4.0)
    return drawn.astype(jnp.bfloat16)


def plant(array, own_key, least, largest):
    index_at = [jax.random.randint(jax.random.fold_in(own_key, axis), (), 0, length) for axis, length in enumerate(array.shape)]
    main_axis = array.shape.index(max(array.shape))
    neighbour = index_at[:main_axis] + [(index_at[main_axis] + 1) % array.shape[main_axis]] + index_at[main_axis + 1:]
    return array.at[tuple(index_at)].set(least).at[tuple(neighbour)].set(largest)


def strengthened(result, key, source, target, parts, factor):
    owner, partner = [(jnp.arange(result.shape[dim]) // (result.shape[dim] // parts)).reshape([-1 if axis == dim else 1 for axis in range(result.ndim)]) for dim in (source, target)]
    chosen = jax.random.permutation(key, parts)[partner]
    strong = (owner == chosen) | (owner == (partner + parts // 2) % parts)
    return jnp.where(strong, factor * result, result)


def steps_of(key, extent, split, low, top_value):
    def one(position, shards_of):
        draws = jax.random.uniform(jax.random.fold_in(jax.random.fold_in(key, 6), position), (shards_of,), jnp.float32, low / len(split), top_value / len(split))
        return jnp.repeat(jnp.exp(draws), extent[position] // shards_of).reshape((-1,) + (1,) * (len(extent) - position - 1))

    factor_of = one(*split[0])
    for cut in split[1:]:
        factor_of = factor_of * one(*cut)
    return factor_of


def scatter_about(rng, shape, deviation, bound, shards=(), held_as=jnp.bfloat16):
    entries = deviation * jax.random.normal(rng, shape, jnp.float32)
    if shards:
        entries = entries * steps_of(rng, shape, shards, -0.22, 0.18)
    return jnp.clip(entries, -bound, bound).astype(held_as)


def heavy_noise(rng, dims, deviation, limit, cuts, heavy, kind=jnp.bfloat16):
    entries = deviation * jax.random.normal(rng, dims, jnp.float32)
    if cuts:
        entries = entries * steps_of(rng, dims, cuts, -0.22, 0.18)
    return jnp.clip(strengthened(entries, jax.random.fold_in(rng, 3), *heavy), -limit, limit).astype(kind)


def setup_inputs(seed: int = 0, part: int = 0) -> dict:
    arg_keys = jax.random.split(jax.random.key(seed), 7)
    own_keys = jax.random.split(jax.random.fold_in(arg_keys[6], part), 7)
    queries = draw_queries(jax.random.fold_in(jax.random.fold_in(arg_keys[6], part), 71), part)
    key_rows = draw_key_rows(jax.random.fold_in(jax.random.fold_in(arg_keys[6], part), 71), part)
    value_rows = scatter_about(own_keys[2], (TOKENS, H * HD), 1.0, 6.0, ((0, 16),))
    out_grad = heavy_noise(own_keys[3], (TOKENS, D), 1.0, 6.0, ((0, 16),), (0, 1, 16, 2.0))
    out_weight = scatter_about(arg_keys[4], (D, H * HD), (H * HD) ** -0.5, 0.1875, ((0, 16),))
    pair_allowed = plant((jax.random.randint(own_keys[5], (NBLK, SPAN), 0, 3) < 2).astype(jnp.int32), jax.random.fold_in(own_keys[5], 1), 0, 1)
    return dict(queries=queries, key_rows=key_rows, value_rows=value_rows, out_grad=out_grad, out_weight=out_weight, pair_allowed=pair_allowed)


def rounded(values):
    return lax.optimization_barrier(values.astype(jnp.bfloat16)).astype(jnp.float32)

def reference(queries, key_rows, value_rows, out_grad, out_weight, pair_allowed):
    num_blocks = BDEV * N_CTX
    feature_width = H * HD
    inv_scale = 1.0 / math.sqrt(HD)
    q_nat = queries.reshape(num_blocks, BLK, H, HD)
    k_nat = key_rows.reshape(num_blocks, BLK, H, HD)
    v_nat = value_rows.reshape(num_blocks, BLK, H, HD)
    offsets = jnp.arange(SPAN + 1, dtype=jnp.int32)
    row_ids = jnp.arange(BLK, dtype=jnp.int32)
    col_ids = jnp.arange((SPAN + 1) * BLK, dtype=jnp.int32)
    col_block = col_ids // BLK
    diagonal = (col_ids[None, :] <= row_ids[:, None]) & (col_block[None, :] == 0)

    def softmax_of(block):
        key_index = jnp.maximum(block - offsets, 0).astype(jnp.int32)
        listed = jnp.concatenate([jnp.ones((1,), bool), pair_allowed[block] > 0])
        valid = (block - offsets >= 0) & listed
        visible = diagonal | valid[col_block][None, :] & (col_block[None, :] > 0)
        keys_sel = k_nat[key_index].reshape((SPAN + 1) * BLK, H, HD)
        values_sel = v_nat[key_index].reshape((SPAN + 1) * BLK, H, HD)
        scores = jnp.einsum('qhd,khd->hqk', q_nat[block].astype(jnp.float32), keys_sel.astype(jnp.float32)) * inv_scale
        safe = jnp.where(visible[None], scores, -1e+30)
        top_score = lax.optimization_barrier(jnp.max(safe, axis=-1, keepdims=True))
        expo = jnp.where(visible[None], jnp.exp(safe - top_score), 0.0)
        probs = expo / lax.optimization_barrier(jnp.sum(expo, axis=-1, keepdims=True))
        return (probs, keys_sel, values_sel, key_index)

    def forward(block):
        probs, keys_sel, values_sel, key_index = softmax_of(block)
        return jnp.einsum('hqk,khd->qhd', rounded(probs), values_sel.astype(jnp.float32))
    context = lax.map(forward, jnp.arange(num_blocks, dtype=jnp.int32))
    attn = context.astype(jnp.bfloat16).reshape(num_blocks * BLK, feature_width)
    layer_out = jnp.dot(attn, out_weight.T, preferred_element_type=jnp.float32).astype(jnp.bfloat16)
    attn_grad = jnp.dot(out_grad, out_weight, preferred_element_type=jnp.float32).astype(jnp.bfloat16)
    weight_grad = jnp.dot(out_grad.T, attn, preferred_element_type=jnp.float32)
    grad_nat = attn_grad.reshape(num_blocks, BLK, H, HD)

    def backward(block):
        probs, keys_sel, values_sel, key_index = softmax_of(block)
        grad_here = grad_nat[block].astype(jnp.float32)
        prob_grad = jnp.einsum('qhd,khd->hqk', grad_here, values_sel.astype(jnp.float32))
        row_delta = jnp.einsum('qhd,qhd->hq', grad_here, context[block])
        score_grad = rounded(probs * (prob_grad - row_delta[:, :, None]) * inv_scale)
        q_part = jnp.einsum('hqk,khd->qhd', score_grad, keys_sel.astype(jnp.float32))
        k_part = jnp.einsum('hqk,qhd->khd', score_grad, q_nat[block].astype(jnp.float32))
        v_part = jnp.einsum('hqk,qhd->khd', rounded(probs), grad_here)
        return (q_part.reshape(BLK, feature_width), k_part.reshape(SPAN + 1, BLK, feature_width), v_part.reshape(SPAN + 1, BLK, feature_width), key_index)
    q_grads, k_parts, v_parts, key_index = lax.map(backward, jnp.arange(num_blocks, dtype=jnp.int32))
    flat_index = key_index.reshape(-1)
    k_total = jnp.zeros((num_blocks, BLK, feature_width), jnp.float32).at[flat_index].add(k_parts.reshape(-1, BLK, feature_width))
    v_total = jnp.zeros((num_blocks, BLK, feature_width), jnp.float32).at[flat_index].add(v_parts.reshape(-1, BLK, feature_width))
    query_grad = q_grads.reshape(num_blocks * BLK, feature_width).astype(jnp.bfloat16)
    key_grad = k_total.reshape(num_blocks * BLK, feature_width).astype(jnp.bfloat16)
    value_grad = v_total.reshape(num_blocks * BLK, feature_width).astype(jnp.bfloat16)
    return (layer_out, query_grad, key_grad, value_grad, weight_grad)
```

```python
import functools
import math

import jax
import jax.numpy as jnp
from jax import lax
from jax.experimental import pallas as pl
from jax.experimental.pallas import tpu as pltpu
from jax.sharding import PartitionSpec as P

H = 8
HD = 128
BLK = 128
SPAN = 2
CHUNK = 256
MESH = pl.DeviceIdType.MESH
F32 = jnp.float32
BF16 = jnp.bfloat16
NEG = -1e30


def dot(a, b, ca, cb):
    return lax.dot_general(a, b, (((ca,), (cb,)), ((), ())), preferred_element_type=F32)


def kernel(
    n,
    pa, q, k, v, og, w,
    lo, qg, kg, vg, wg,
    wbuf, part, from_core, y_out, y_in, z_out, z_in,
    k_halo, v_halo, dk_out, dv_out, dk_in, dv_in, dk_own, dv_own,
    probs_buf, ctx_buf, attn, da, bias,
    w_send, w_recv, halo_send, halo_recv, back_send, back_recv,
    c_send, c_recv, y_send, y_recv, z_send, z_recv,
):
    g = lax.axis_index("groups")
    me = lax.axis_index("ctx")
    zs = n // 4
    rows = q.shape[0]
    half = q.shape[1] // 2
    depth = w.shape[0]
    per_chunk = CHUNK // depth
    chunks = og.shape[1] // CHUNK
    core = lax.rem(me, 2)
    chip = me // 2
    y = lax.rem(chip, 2)
    z = chip // 2
    hm = lax.rem(g, 2)
    ho = 1 - hm
    inv_scale = 1.0 / math.sqrt(HD)

    def index(zz, yy, cc):
        return (zz * 2 + yy) * 2 + cc

    sib = (g, index(z, y, 1 - core))
    ypeer = (g, index(z, 1 - y, core))
    xpeer = (g + 1 - 2 * hm, me)
    up = (g, lax.rem(me + 1, n))
    down = (g, lax.rem(me + n - 1, n))

    def rc(src, dst, ss, rs, dev):
        return pltpu.make_async_remote_copy(
            src_ref=src, dst_ref=dst, send_sem=ss, recv_sem=rs,
            device_id=dev, device_id_type=MESH,
        )

    barrier = pltpu.get_barrier_semaphore()
    for dev in (sib, ypeer, xpeer, up, down):
        pl.semaphore_signal(barrier, inc=1, device_id=dev, device_id_type=MESH)
    for step in range(1, zs):
        dev = (g, index(lax.rem(z + step, zs), y, core))
        pl.semaphore_signal(barrier, inc=1, device_id=dev, device_id_type=MESH)

    wbuf[0, me] = w[:, :half]
    wbuf[1, me] = w[:, half:]
    pl.semaphore_wait(barrier, 5 + zs - 1)

    def halo(i, part_of):
        src, dst = ((k, k_halo), (v, v_halo))[part_of]
        return rc(src.at[:, pl.ds(i * half, half)], dst.at[i],
                  halo_send.at[2 * i + part_of], halo_recv.at[2 * i + part_of], up)

    @pl.when(me < n - 1)
    def _():
        for i in range(2):
            for part_of in range(2):
                halo(i, part_of).start()

    def w_copy(kind, h, idx, dev):
        return rc(wbuf.at[h, idx], wbuf.at[h, idx], w_send.at[kind, h, idx], w_recv.at[h, idx], dev)

    def z_own(step):
        dev = (g, index(lax.rem(z + step, zs), y, core))
        return rc(wbuf.at[hm, me], wbuf.at[hm, me], w_send.at[3, 0, step], w_recv.at[hm, me], dev)

    def start_z(step, c):
        z_own(step).start()
        return c

    lax.fori_loop(1, zs, start_z, 0)
    w_copy(0, hm, me, ypeer).start()
    w_copy(2, 0, me, sib).start()
    w_copy(2, 1, me, sib).start()

    row_ids = lax.broadcasted_iota(jnp.int32, (BLK, BLK), 0)
    col_ids = lax.broadcasted_iota(jnp.int32, (BLK, BLK), 1)
    count = rows // BLK
    for a in range(count):
        blk = me * count + a
        for e in range(count + SPAN):
            back = a + SPAN - e
            if back == 0:
                tile = jnp.where(col_ids <= row_ids, 0.0, NEG)
            elif 0 < back <= SPAN:
                ok = pa[blk, back - 1] * jnp.where(blk >= back, 1, 0)
                tile = jnp.where(jnp.full((BLK, BLK), ok, jnp.int32) > 0, 0.0, NEG)
            else:
                tile = jnp.full((BLK, BLK), NEG, F32)
            bias[a * BLK:(a + 1) * BLK, e * BLK:(e + 1) * BLK] = tile

    def from_z(step, c):
        idx = index(lax.rem(z + step, zs), y, core)
        w_copy(0, hm, idx, ypeer).wait_recv()
        w_copy(0, hm, idx, ypeer).start()
        w_copy(1, hm, idx, xpeer).start()
        w_copy(2, hm, idx, sib).start()
        return c

    lax.fori_loop(1, zs, from_z, 0)

    @pl.when(me == 0)
    def _():
        k_halo[...] = jnp.zeros_like(k_halo)
        v_halo[...] = jnp.zeros_like(v_halo)

    def ext(ref, halo_ref, i, j):
        at = pl.ds(pl.multiple_of(j * HD, HD), HD)
        own = pl.ds(pl.multiple_of(i * half + j * HD, HD), HD)
        return jnp.concatenate([halo_ref[i, :, at], ref[:, own]], axis=0), own

    for i in range(2):
        @pl.when(me > 0)
        def _():
            for part_of in range(2):
                halo(i, part_of).wait_recv()

        def forward(j, c):
            keys, own = ext(k, k_halo, i, j)
            values, _ = ext(v, v_halo, i, j)
            s = dot(q[:, own], keys, 1, 1) * inv_scale + bias[...]
            e = jnp.exp(s - jnp.max(s, axis=-1, keepdims=True))
            probs = e * (1.0 / jnp.sum(e, axis=-1, keepdims=True))
            probs_buf[i * (H // 2) + j] = probs
            context = dot(probs.astype(BF16), values, 1, 0)
            ctx_buf[:, own] = context
            attn[:, own] = context.astype(BF16)
            return c

        lax.fori_loop(0, H // 2, forward, 0)

    def c_copy(o):
        return rc(part.at[o * 2 + 1 - core], from_core.at[o], c_send.at[o], c_recv.at[o], sib)

    def share(t, c):
        j = lax.rem(t + 1 + (z * 2 * depth * 2) // CHUNK, chunks)
        cols = pl.ds(pl.multiple_of(j * CHUNK, CHUNK), CHUNK)
        r = dot(og[:, cols], attn[...], 0, 0).astype(BF16)
        part[pl.ds(j * per_chunk, per_chunk)] = r.reshape(per_chunk, depth, 2 * half)
        for b in range(per_chunk // 2):
            c_copy(j * (per_chunk // 2) + b).start()
        return c

    lax.fori_loop(0, chunks, share, 0)

    def y_copy(zz):
        return rc(y_out.at[zz], y_in.at[zz], y_send.at[zz], y_recv.at[zz], ypeer)

    def stage_y(step, c):
        zz = lax.rem(z + step, zs)
        o = zz * 2 + 1 - y
        c_copy(o).wait_recv()
        y_out[zz] = (part[o * 2 + core].astype(F32) + from_core[o].astype(F32)).astype(BF16)
        y_copy(zz).start()
        return c

    lax.fori_loop(1, zs + 1, stage_y, 0)

    def from_y(step, c):
        idx = index(lax.rem(z + step, zs), 1 - y, core)
        w_copy(0, hm, idx, xpeer).wait_recv()
        w_copy(1, hm, idx, xpeer).start()
        w_copy(2, hm, idx, sib).start()
        return c

    lax.fori_loop(0, zs, from_y, 0)

    def from_x(step, c):
        for yy in range(2):
            idx = index(lax.rem(z + step, zs), (y, 1 - y)[yy], core)

            def go(idx=idx):
                w_copy(1, ho, idx, xpeer).wait_recv()
                w_copy(2, ho, idx, sib).start()

            if yy == 0:
                pl.when(step > 0)(go)
            else:
                go()
        return c

    lax.fori_loop(0, zs, from_x, 0)

    def from_sib(o, c):
        for h in range(2):
            w_copy(2, h, o * 2 + 1 - core, sib).wait_recv()
        return c

    lax.fori_loop(0, n // 2, from_sib, 0)

    for h in range(2):
        for part_of in range(half // CHUNK):
            cols = slice(part_of * CHUNK, (part_of + 1) * CHUNK)
            r = dot(og[...], wbuf[h, :, :, cols].reshape(n * depth, CHUNK), 1, 0)
            da[:, h * half + part_of * CHUNK:h * half + (part_of + 1) * CHUNK] = r.astype(BF16)

    def back_copy(i, part_of):
        src, dst = ((dk_out, dk_in), (dv_out, dv_in))[part_of]
        at = 2 * i + part_of
        return rc(src.at[i], dst.at[i], back_send.at[at], back_recv.at[at], down)

    for i in range(2):
        def backward(j, c):
            keys, own = ext(k, k_halo, i, j)
            values, _ = ext(v, v_halo, i, j)
            at = pl.ds(pl.multiple_of(j * HD, HD), HD)
            d = da[:, own]
            probs = probs_buf[i * (H // 2) + j]
            delta = jnp.sum(d.astype(F32) * ctx_buf[:, own], axis=-1, keepdims=True)
            sg = (probs * (dot(d, values, 1, 1) - delta) * inv_scale).astype(BF16)
            dk = dot(sg, q[:, own], 0, 0)
            dv = dot(probs.astype(BF16), d, 0, 0)
            dk_out[i, :, at] = dk[:rows].astype(BF16)
            dv_out[i, :, at] = dv[:rows].astype(BF16)
            dk_own[:, own] = dk[rows:]
            dv_own[:, own] = dv[rows:]
            qg[:, own] = dot(sg, keys, 1, 0).astype(BF16)
            return c

        lax.fori_loop(0, H // 2, backward, 0)

        @pl.when(me > 0)
        def _():
            for part_of in range(2):
                back_copy(i, part_of).start()

    def z_copy(zz, slot):
        return rc(z_out.at[zz], z_in.at[slot], z_send.at[zz], z_recv.at[slot], (g, index(zz, y, core)))

    def summed(zz):
        o = zz * 2 + y
        c_copy(o).wait_recv()
        y_copy(zz).wait_recv()
        return part[o * 2 + core].astype(F32) + from_core[o].astype(F32) + y_in[zz].astype(F32)

    def stage_z(step, c):
        zz = lax.rem(z + step, zs)
        z_out[zz] = summed(zz).astype(BF16)
        z_copy(zz, z).start()
        return c

    lax.fori_loop(1, zs, stage_z, 0)

    def layer(j, c):
        rows_of = pl.ds(j * per_chunk, per_chunk)
        r = dot(attn[:, :half], wbuf[0, rows_of].reshape(CHUNK, half), 1, 1)
        r = r + dot(attn[:, half:], wbuf[1, rows_of].reshape(CHUNK, half), 1, 1)
        lo[:, pl.ds(pl.multiple_of(j * CHUNK, CHUNK), CHUNK)] = r.astype(BF16)
        return c

    lax.fori_loop(0, chunks, layer, 0)

    wg[...] = summed(z)

    for i in range(2):
        cols = slice(i * half, (i + 1) * half)

        @pl.when(me < n - 1)
        def _():
            for part_of in range(2):
                back_copy(i, part_of).wait_recv()
            kg[:, cols] = (dk_own[:, cols] + dk_in[i].astype(F32)).astype(BF16)
            vg[:, cols] = (dv_own[:, cols] + dv_in[i].astype(F32)).astype(BF16)

        @pl.when(me == n - 1)
        def _():
            kg[:, cols] = dk_own[:, cols].astype(BF16)
            vg[:, cols] = dv_own[:, cols].astype(BF16)

    def last(step, c):
        zz = lax.rem(z + step, zs)
        z_copy(zz, zz).wait_recv()
        wg[...] += z_in[zz].astype(F32)
        return c

    lax.fori_loop(1, zs, last, 0)

    @pl.when(me < n - 1)
    def _():
        for i in range(2):
            for part_of in range(2):
                halo(i, part_of).wait_send()

    @pl.when(me > 0)
    def _():
        for i in range(2):
            for part_of in range(2):
                back_copy(i, part_of).wait_send()

    def sent(step, c):
        zz = lax.rem(z + step, zs)
        mine = index(zz, y, core)
        other = index(zz, 1 - y, core)
        w_copy(0, hm, mine, ypeer).wait_send()
        w_copy(1, hm, other, xpeer).wait_send()
        w_copy(2, hm, mine, sib).wait_send()
        w_copy(2, ho, mine, sib).wait_send()
        w_copy(2, hm, other, sib).wait_send()
        w_copy(2, ho, other, sib).wait_send()
        y_copy(zz).wait_send()
        c_copy(zz * 2).wait_send()
        c_copy(zz * 2 + 1).wait_send()

        @pl.when(step > 0)
        def _():
            z_own(step).wait_send()
            w_copy(1, hm, mine, xpeer).wait_send()
            z_copy(zz, z).wait_send()

        return c

    lax.fori_loop(0, zs, sent, 0)


def per_device(n, queries, key_rows, value_rows, out_grad, out_weight, pair_allowed):
    rows, width = queries.shape
    model = out_grad.shape[1]
    depth = out_weight.shape[0]
    zs = n // 4
    half = width // 2
    vmem = pl.BlockSpec(memory_space=pltpu.VMEM)
    dma = pltpu.SemaphoreType.DMA
    return pl.pallas_call(
        functools.partial(kernel, n),
        out_shape=(
            jax.ShapeDtypeStruct((rows, model), BF16),
            jax.ShapeDtypeStruct((rows, width), BF16),
            jax.ShapeDtypeStruct((rows, width), BF16),
            jax.ShapeDtypeStruct((rows, width), BF16),
            jax.ShapeDtypeStruct((depth, width), F32),
        ),
        in_specs=[pl.BlockSpec(memory_space=pltpu.SMEM)] + [vmem] * 5,
        out_specs=(vmem,) * 5,
        scratch_shapes=[
            pltpu.VMEM((2, n, depth, half), BF16),
            pltpu.VMEM((n, depth, width), BF16),
            pltpu.VMEM((n // 2, depth, width), BF16),
            pltpu.VMEM((zs, depth, width), BF16),
            pltpu.VMEM((zs, depth, width), BF16),
            pltpu.VMEM((zs, depth, width), BF16),
            pltpu.VMEM((zs, depth, width), BF16),
        ]
        + [pltpu.VMEM((2, rows, half), BF16)] * 6
        + [
            pltpu.VMEM((rows, width), F32),
            pltpu.VMEM((rows, width), F32),
            pltpu.VMEM((H, rows, rows + SPAN * BLK), F32),
            pltpu.VMEM((rows, width), F32),
            pltpu.VMEM((rows, width), BF16),
            pltpu.VMEM((rows, width), BF16),
            pltpu.VMEM((rows, rows + SPAN * BLK), F32),
            dma((4, 2, n)),
            dma((2, n)),
            dma((4,)), dma((4,)), dma((4,)), dma((4,)),
            dma((n // 2,)), dma((n // 2,)),
            dma((zs,)), dma((zs,)), dma((zs,)), dma((zs,)),
        ],
        compiler_params=pltpu.CompilerParams(
            collective_id=0, has_side_effects=True, vmem_limit_bytes=52 * 2**20
        ),
    )(pair_allowed, queries, key_rows, value_rows, out_grad, out_weight)


def solution(mesh):
    both = P(("groups", "ctx"), None)
    return jax.shard_map(
        functools.partial(per_device, mesh.shape["ctx"]),
        mesh=mesh,
        in_specs=(both, both, both, both, P("ctx", None), P("groups", None)),
        out_specs=(both,) * 5,
        check_vma=False,
    )
```

```python
import functools
import math

import jax
import jax.numpy as jnp
from jax import lax
from jax.experimental import pallas as pl
from jax.experimental.pallas import tpu as pltpu
from jax.sharding import PartitionSpec as P

H = 8
HD = 128
BLK = 128
SPAN = 2
CHUNK = 256
MESH = pl.DeviceIdType.MESH
F32 = jnp.float32
BF16 = jnp.bfloat16
NEG = -1e30


def dot(a, b, ca, cb):
    return lax.dot_general(a, b, (((ca,), (cb,)), ((), ())), preferred_element_type=F32)


def kernel(
    n,
    pa, q, k, v, og, w,
    lo, qg, kg, vg, wg,
    wbuf, part, from_core, y_out, y_in, z_out, z_in,
    k_halo, v_halo, dk_out, dv_out, dk_in, dv_in, dk_own, dv_own,
    probs_buf, ctx_buf, attn, da, bias,
    w_send, w_recv, halo_send, halo_recv, back_send, back_recv,
    c_send, c_recv, y_send, y_recv, z_send, z_recv,
):
    g = lax.axis_index("groups")
    me = lax.axis_index("ctx")
    zs = n // 4
    rows = q.shape[0]
    half = q.shape[1] // 2
    depth = w.shape[0]
    per_chunk = CHUNK // depth
    chunks = og.shape[1] // CHUNK
    core = lax.rem(me, 2)
    chip = me // 2
    y = lax.rem(chip, 2)
    z = chip // 2
    hm = lax.rem(g, 2)
    ho = 1 - hm
    inv_scale = 1.0 / math.sqrt(HD)

    def index(zz, yy, cc):
        return (zz * 2 + yy) * 2 + cc

    sib = (g, index(z, y, 1 - core))
    ypeer = (g, index(z, 1 - y, core))
    xpeer = (g + 1 - 2 * hm, me)
    up = (g, lax.rem(me + 1, n))
    down = (g, lax.rem(me + n - 1, n))

    def rc(src, dst, ss, rs, dev):
        return pltpu.make_async_remote_copy(
            src_ref=src, dst_ref=dst, send_sem=ss, recv_sem=rs,
            device_id=dev, device_id_type=MESH,
        )

    barrier = pltpu.get_barrier_semaphore()
    for dev in (sib, ypeer, xpeer, up, down):
        pl.semaphore_signal(barrier, inc=1, device_id=dev, device_id_type=MESH)
    for step in range(1, zs):
        dev = (g, index(lax.rem(z + step, zs), y, core))
        pl.semaphore_signal(barrier, inc=1, device_id=dev, device_id_type=MESH)

    wbuf[0, me] = w[:, :half]
    wbuf[1, me] = w[:, half:]
    pl.semaphore_wait(barrier, 5 + zs - 1)

    def halo(i, part_of):
        src, dst = ((k, k_halo), (v, v_halo))[part_of]
        return rc(src.at[:, pl.ds(i * half, half)], dst.at[i],
                  halo_send.at[2 * i + part_of], halo_recv.at[2 * i + part_of], up)

    @pl.when(me < n - 1)
    def _():
        for i in range(2):
            for part_of in range(2):
                halo(i, part_of).start()

    def w_copy(kind, h, idx, dev):
        return rc(wbuf.at[h, idx], wbuf.at[h, idx], w_send.at[kind, h, idx], w_recv.at[h, idx], dev)

    def z_own(step):
        dev = (g, index(lax.rem(z + step, zs), y, core))
        return rc(wbuf.at[hm, me], wbuf.at[hm, me], w_send.at[3, 0, step], w_recv.at[hm, me], dev)

    def start_z(step, c):
        z_own(step).start()
        return c

    lax.fori_loop(1, zs, start_z, 0)
    w_copy(2, 0, me, sib).start()
    w_copy(2, 1, me, sib).start()

    row_ids = lax.broadcasted_iota(jnp.int32, (BLK, BLK), 0)
    col_ids = lax.broadcasted_iota(jnp.int32, (BLK, BLK), 1)
    count = rows // BLK
    for a in range(count):
        blk = me * count + a
        for e in range(count + SPAN):
            back = a + SPAN - e
            if back == 0:
                tile = jnp.where(col_ids <= row_ids, 0.0, NEG)
            elif 0 < back <= SPAN:
                ok = pa[blk, back - 1] * jnp.where(blk >= back, 1, 0)
                tile = jnp.where(jnp.full((BLK, BLK), ok, jnp.int32) > 0, 0.0, NEG)
            else:
                tile = jnp.full((BLK, BLK), NEG, F32)
            bias[a * BLK:(a + 1) * BLK, e * BLK:(e + 1) * BLK] = tile

    def from_z(step, c):
        idx = index(lax.rem(z + step, zs), y, core)
        w_copy(0, hm, idx, ypeer).wait_recv()
        w_copy(0, hm, idx, ypeer).start()
        w_copy(1, hm, idx, xpeer).start()
        w_copy(2, hm, idx, sib).start()
        return c

    @pl.when(me == 0)
    def _():
        k_halo[...] = jnp.zeros_like(k_halo)
        v_halo[...] = jnp.zeros_like(v_halo)

    def ext(ref, halo_ref, i, j):
        at = pl.ds(pl.multiple_of(j * HD, HD), HD)
        own = pl.ds(pl.multiple_of(i * half + j * HD, HD), HD)
        return jnp.concatenate([halo_ref[i, :, at], ref[:, own]], axis=0), own

    def from_y(step, c):
        idx = index(lax.rem(z + step, zs), 1 - y, core)
        w_copy(0, hm, idx, xpeer).wait_recv()
        w_copy(1, hm, idx, xpeer).start()
        w_copy(2, hm, idx, sib).start()
        return c

    def from_x(yy):
        def go(step, c):
            idx = index(lax.rem(z + step, zs), yy, core)
            w_copy(1, ho, idx, xpeer).wait_recv()
            w_copy(2, ho, idx, sib).start()
            return c

        return go

    def from_sib(h):
        def go(o, c):
            w_copy(2, h, o * 2 + 1 - core, sib).wait_recv()
            return c

        return go

    for i in range(2):
        @pl.when(me > 0)
        def _():
            for part_of in range(2):
                halo(i, part_of).wait_recv()

        def forward(j, c):
            keys, own = ext(k, k_halo, i, j)
            values, _ = ext(v, v_halo, i, j)
            s = dot(q[:, own], keys, 1, 1) * inv_scale + bias[...]
            e = jnp.exp(s - jnp.max(s, axis=-1, keepdims=True))
            probs = e * (1.0 / jnp.sum(e, axis=-1, keepdims=True))
            probs_buf[i * (H // 2) + j] = probs
            context = dot(probs.astype(BF16), values, 1, 0)
            ctx_buf[:, own] = context
            attn[:, own] = context.astype(BF16)
            return c

        lax.fori_loop(0, H // 2, forward, 0)
        if i == 0:
            w_copy(0, hm, me, ypeer).start()
            lax.fori_loop(1, zs, from_z, 0)
        else:
            lax.fori_loop(1, zs, from_x(y), 0)

    def c_copy(o):
        return rc(part.at[o * 2 + 1 - core], from_core.at[o], c_send.at[o], c_recv.at[o], sib)

    def share(t, c):
        j = lax.rem(t + 1 + (z * 2 * depth * 2) // CHUNK, chunks)
        cols = pl.ds(pl.multiple_of(j * CHUNK, CHUNK), CHUNK)
        r = dot(og[:, cols], attn[...], 0, 0).astype(BF16)
        part[pl.ds(j * per_chunk, per_chunk)] = r.reshape(per_chunk, depth, 2 * half)
        for b in range(per_chunk // 2):
            c_copy(j * (per_chunk // 2) + b).start()
        lax.fori_loop((t * zs) // chunks, ((t + 1) * zs) // chunks, from_y, 0)
        return c

    lax.fori_loop(0, chunks, share, 0)

    def y_copy(zz):
        return rc(y_out.at[zz], y_in.at[zz], y_send.at[zz], y_recv.at[zz], ypeer)

    def stage_y(step, c):
        zz = lax.rem(z + step, zs)
        o = zz * 2 + 1 - y
        c_copy(o).wait_recv()
        y_out[zz] = (part[o * 2 + core].astype(F32) + from_core[o].astype(F32)).astype(BF16)
        y_copy(zz).start()
        return c

    lax.fori_loop(1, zs + 1, stage_y, 0)

    def attn_grad(h):
        for part_of in range(half // CHUNK):
            cols = slice(part_of * CHUNK, (part_of + 1) * CHUNK)
            r = dot(og[...], wbuf[h, :, :, cols].reshape(n * depth, CHUNK), 1, 0)
            at = pl.ds(pl.multiple_of(h * half + part_of * CHUNK, CHUNK), CHUNK)
            da[:, at] = r.astype(BF16)

    def back_copy(i, part_of):
        src, dst = ((dk_out, dk_in), (dv_out, dv_in))[part_of]
        at = 2 * i + part_of
        return rc(src.at[i], dst.at[i], back_send.at[at], back_recv.at[at], down)

    def backward_half(i):
        def backward(j, c):
            keys, own = ext(k, k_halo, i, j)
            values, _ = ext(v, v_halo, i, j)
            at = pl.ds(pl.multiple_of(j * HD, HD), HD)
            d = da[:, own]
            probs = probs_buf[i * (H // 2) + j]
            delta = jnp.sum(d.astype(F32) * ctx_buf[:, own], axis=-1, keepdims=True)
            sg = (probs * (dot(d, values, 1, 1) - delta) * inv_scale).astype(BF16)
            dk = dot(sg, q[:, own], 0, 0)
            dv = dot(probs.astype(BF16), d, 0, 0)
            dk_out[i, :, at] = dk[:rows].astype(BF16)
            dv_out[i, :, at] = dv[:rows].astype(BF16)
            dk_own[:, own] = dk[rows:]
            dv_own[:, own] = dv[rows:]
            qg[:, own] = dot(sg, keys, 1, 0).astype(BF16)
            return c

        lax.fori_loop(0, H // 2, backward, 0)

        @pl.when(me > 0)
        def _():
            for part_of in range(2):
                back_copy(i, part_of).start()

    def z_copy(zz, slot):
        return rc(z_out.at[zz], z_in.at[slot], z_send.at[zz], z_recv.at[slot], (g, index(zz, y, core)))

    def summed(zz):
        o = zz * 2 + y
        c_copy(o).wait_recv()
        y_copy(zz).wait_recv()
        return part[o * 2 + core].astype(F32) + from_core[o].astype(F32) + y_in[zz].astype(F32)

    def stage_z(step, c):
        zz = lax.rem(z + step, zs)
        z_out[zz] = summed(zz).astype(BF16)
        z_copy(zz, z).start()
        return c

    early = 1 + zs // 2
    lax.fori_loop(0, n // 2, from_sib(hm), 0)
    attn_grad(hm)
    backward_half(hm)
    lax.fori_loop(1, early, stage_z, 0)
    lax.fori_loop(0, zs, from_x(1 - y), 0)
    lax.fori_loop(0, n // 2, from_sib(ho), 0)
    attn_grad(ho)
    backward_half(ho)
    lax.fori_loop(early, zs, stage_z, 0)

    def layer(j, c):
        rows_of = pl.ds(j * per_chunk, per_chunk)
        r = dot(attn[:, :half], wbuf[0, rows_of].reshape(CHUNK, half), 1, 1)
        r = r + dot(attn[:, half:], wbuf[1, rows_of].reshape(CHUNK, half), 1, 1)
        lo[:, pl.ds(pl.multiple_of(j * CHUNK, CHUNK), CHUNK)] = r.astype(BF16)
        return c

    lax.fori_loop(0, chunks, layer, 0)

    wg[...] = summed(z)

    for i in range(2):
        cols = slice(i * half, (i + 1) * half)

        @pl.when(me < n - 1)
        def _():
            for part_of in range(2):
                back_copy(i, part_of).wait_recv()
            kg[:, cols] = (dk_own[:, cols] + dk_in[i].astype(F32)).astype(BF16)
            vg[:, cols] = (dv_own[:, cols] + dv_in[i].astype(F32)).astype(BF16)

        @pl.when(me == n - 1)
        def _():
            kg[:, cols] = dk_own[:, cols].astype(BF16)
            vg[:, cols] = dv_own[:, cols].astype(BF16)

    def last(step, c):
        zz = lax.rem(z + step, zs)
        z_copy(zz, zz).wait_recv()
        wg[...] += z_in[zz].astype(F32)
        return c

    lax.fori_loop(1, zs, last, 0)

    @pl.when(me < n - 1)
    def _():
        for i in range(2):
            for part_of in range(2):
                halo(i, part_of).wait_send()

    @pl.when(me > 0)
    def _():
        for i in range(2):
            for part_of in range(2):
                back_copy(i, part_of).wait_send()

    def sent(step, c):
        zz = lax.rem(z + step, zs)
        mine = index(zz, y, core)
        other = index(zz, 1 - y, core)
        w_copy(0, hm, mine, ypeer).wait_send()
        w_copy(1, hm, other, xpeer).wait_send()
        w_copy(2, hm, mine, sib).wait_send()
        w_copy(2, ho, mine, sib).wait_send()
        w_copy(2, hm, other, sib).wait_send()
        w_copy(2, ho, other, sib).wait_send()
        y_copy(zz).wait_send()
        c_copy(zz * 2).wait_send()
        c_copy(zz * 2 + 1).wait_send()

        @pl.when(step > 0)
        def _():
            z_own(step).wait_send()
            w_copy(1, hm, mine, xpeer).wait_send()
            z_copy(zz, z).wait_send()

        return c

    lax.fori_loop(0, zs, sent, 0)


def per_device(n, queries, key_rows, value_rows, out_grad, out_weight, pair_allowed):
    rows, width = queries.shape
    model = out_grad.shape[1]
    depth = out_weight.shape[0]
    zs = n // 4
    half = width // 2
    vmem = pl.BlockSpec(memory_space=pltpu.VMEM)
    dma = pltpu.SemaphoreType.DMA
    return pl.pallas_call(
        functools.partial(kernel, n),
        out_shape=(
            jax.ShapeDtypeStruct((rows, model), BF16),
            jax.ShapeDtypeStruct((rows, width), BF16),
            jax.ShapeDtypeStruct((rows, width), BF16),
            jax.ShapeDtypeStruct((rows, width), BF16),
            jax.ShapeDtypeStruct((depth, width), F32),
        ),
        in_specs=[pl.BlockSpec(memory_space=pltpu.SMEM)] + [vmem] * 5,
        out_specs=(vmem,) * 5,
        scratch_shapes=[
            pltpu.VMEM((2, n, depth, half), BF16),
            pltpu.VMEM((n, depth, width), BF16),
            pltpu.VMEM((n // 2, depth, width), BF16),
            pltpu.VMEM((zs, depth, width), BF16),
            pltpu.VMEM((zs, depth, width), BF16),
            pltpu.VMEM((zs, depth, width), BF16),
            pltpu.VMEM((zs, depth, width), BF16),
        ]
        + [pltpu.VMEM((2, rows, half), BF16)] * 6
        + [
            pltpu.VMEM((rows, width), F32),
            pltpu.VMEM((rows, width), F32),
            pltpu.VMEM((H, rows, rows + SPAN * BLK), F32),
            pltpu.VMEM((rows, width), F32),
            pltpu.VMEM((rows, width), BF16),
            pltpu.VMEM((rows, width), BF16),
            pltpu.VMEM((rows, rows + SPAN * BLK), F32),
            dma((4, 2, n)),
            dma((2, n)),
            dma((4,)), dma((4,)), dma((4,)), dma((4,)),
            dma((n // 2,)), dma((n // 2,)),
            dma((zs,)), dma((zs,)), dma((zs,)), dma((zs,)),
        ],
        compiler_params=pltpu.CompilerParams(
            collective_id=0, has_side_effects=True, vmem_limit_bytes=52 * 2**20
        ),
    )(pair_allowed, queries, key_rows, value_rows, out_grad, out_weight)


def solution(mesh):
    both = P(("groups", "ctx"), None)
    return jax.shard_map(
        functools.partial(per_device, mesh.shape["ctx"]),
        mesh=mesh,
        in_specs=(both, both, both, both, P("ctx", None), P("groups", None)),
        out_specs=(both,) * 5,
        check_vma=False,
    )
```

```python
import functools
import math

import jax
import jax.numpy as jnp
from jax import lax
from jax.experimental import pallas as pl
from jax.experimental.pallas import tpu as pltpu
from jax.sharding import PartitionSpec as P

H = 8
HD = 128
BLK = 128
SPAN = 2
CHUNK = 256
MESH = pl.DeviceIdType.MESH
F32 = jnp.float32
BF16 = jnp.bfloat16
NEG = -1e30


def dot(a, b, ca, cb):
    return lax.dot_general(a, b, (((ca,), (cb,)), ((), ())), preferred_element_type=F32)


def kernel(
    n,
    pa, q, k, v, og, w,
    lo, qg, kg, vg, wg,
    wbuf, part, from_core, y_out, y_in, z_out, z_in,
    k_halo, v_halo, dk_out, dv_out, dk_in, dv_in, dk_own, dv_own,
    probs_buf, ctx_buf, attn, da, bias,
    w_send, w_recv, halo_send, halo_recv, back_send, back_recv,
    c_send, c_recv, y_send, y_recv, z_send, z_recv,
):
    g = lax.axis_index("groups")
    me = lax.axis_index("ctx")
    zs = n // 4
    rows = q.shape[0]
    half = q.shape[1] // 2
    depth = w.shape[0]
    per_chunk = CHUNK // depth
    chunks = og.shape[1] // CHUNK
    core = lax.rem(me, 2)
    chip = me // 2
    y = lax.rem(chip, 2)
    z = chip // 2
    hm = lax.rem(g, 2)
    ho = 1 - hm
    inv_scale = 1.0 / math.sqrt(HD)

    def index(zz, yy, cc):
        return (zz * 2 + yy) * 2 + cc

    sib = (g, index(z, y, 1 - core))
    ypeer = (g, index(z, 1 - y, core))
    xpeer = (g + 1 - 2 * hm, me)
    up = (g, lax.rem(me + 1, n))
    down = (g, lax.rem(me + n - 1, n))

    def rc(src, dst, ss, rs, dev):
        return pltpu.make_async_remote_copy(
            src_ref=src, dst_ref=dst, send_sem=ss, recv_sem=rs,
            device_id=dev, device_id_type=MESH,
        )

    barrier = pltpu.get_barrier_semaphore()
    for dev in (sib, ypeer, xpeer, up, down):
        pl.semaphore_signal(barrier, inc=1, device_id=dev, device_id_type=MESH)
    for step in range(1, zs):
        dev = (g, index(lax.rem(z + step, zs), y, core))
        pl.semaphore_signal(barrier, inc=1, device_id=dev, device_id_type=MESH)

    wbuf[0, me] = w[:, :half]
    wbuf[1, me] = w[:, half:]
    pl.semaphore_wait(barrier, 5 + zs - 1)

    def halo(i, part_of):
        src, dst = ((k, k_halo), (v, v_halo))[part_of]
        return rc(src.at[:, pl.ds(i * half, half)], dst.at[i],
                  halo_send.at[2 * i + part_of], halo_recv.at[2 * i + part_of], up)

    @pl.when(me < n - 1)
    def _():
        for i in range(2):
            for part_of in range(2):
                halo(i, part_of).start()

    def w_copy(kind, h, idx, dev):
        return rc(wbuf.at[h, idx], wbuf.at[h, idx], w_send.at[kind, h, idx], w_recv.at[h, idx], dev)

    def z_own(step):
        dev = (g, index(lax.rem(z + step, zs), y, core))
        return rc(wbuf.at[hm, me], wbuf.at[hm, me], w_send.at[3, 0, step], w_recv.at[hm, me], dev)

    def start_z(step, c):
        z_own(step).start()
        return c

    lax.fori_loop(1, zs, start_z, 0)
    w_copy(0, hm, me, ypeer).start()
    w_copy(2, 0, me, sib).start()
    w_copy(2, 1, me, sib).start()

    row_ids = lax.broadcasted_iota(jnp.int32, (BLK, BLK), 0)
    col_ids = lax.broadcasted_iota(jnp.int32, (BLK, BLK), 1)
    count = rows // BLK
    for a in range(count):
        blk = me * count + a
        for e in range(count + SPAN):
            back = a + SPAN - e
            if back == 0:
                tile = jnp.where(col_ids <= row_ids, 0.0, NEG)
            elif 0 < back <= SPAN:
                ok = pa[blk, back - 1] * jnp.where(blk >= back, 1, 0)
                tile = jnp.where(jnp.full((BLK, BLK), ok, jnp.int32) > 0, 0.0, NEG)
            else:
                tile = jnp.full((BLK, BLK), NEG, F32)
            bias[a * BLK:(a + 1) * BLK, e * BLK:(e + 1) * BLK] = tile

    def from_z(step, c):
        idx = index(lax.rem(z + step, zs), y, core)
        w_copy(0, hm, idx, ypeer).wait_recv()
        w_copy(0, hm, idx, ypeer).start()
        w_copy(1, hm, idx, xpeer).start()
        w_copy(2, hm, idx, sib).start()
        return c

    @pl.when(me == 0)
    def _():
        k_halo[...] = jnp.zeros_like(k_halo)
        v_halo[...] = jnp.zeros_like(v_halo)

    def ext(ref, halo_ref, i, j):
        at = pl.ds(pl.multiple_of(j * HD, HD), HD)
        own = pl.ds(pl.multiple_of(i * half + j * HD, HD), HD)
        return jnp.concatenate([halo_ref[i, :, at], ref[:, own]], axis=0), own

    def from_y(step, c):
        idx = index(lax.rem(z + step, zs), 1 - y, core)
        w_copy(0, hm, idx, xpeer).wait_recv()
        w_copy(1, hm, idx, xpeer).start()
        w_copy(2, hm, idx, sib).start()
        return c

    def from_x(yy):
        def go(step, c):
            idx = index(lax.rem(z + step, zs), yy, core)
            w_copy(1, ho, idx, xpeer).wait_recv()
            w_copy(2, ho, idx, sib).start()
            return c

        return go

    def from_sib(h):
        def go(o, c):
            w_copy(2, h, o * 2 + 1 - core, sib).wait_recv()
            return c

        return go

    for i in range(2):
        @pl.when(me > 0)
        def _():
            for part_of in range(2):
                halo(i, part_of).wait_recv()

        def forward(j, c):
            keys, own = ext(k, k_halo, i, j)
            values, _ = ext(v, v_halo, i, j)
            s = dot(q[:, own], keys, 1, 1) * inv_scale + bias[...]
            e = jnp.exp(s - jnp.max(s, axis=-1, keepdims=True))
            probs = e * (1.0 / jnp.sum(e, axis=-1, keepdims=True))
            probs_buf[i * (H // 2) + j] = probs
            context = dot(probs.astype(BF16), values, 1, 0)
            ctx_buf[:, own] = context
            attn[:, own] = context.astype(BF16)
            return c

        lax.fori_loop(0, H // 2, forward, 0)
        if i == 0:
            lax.fori_loop(1, zs, from_z, 0)
        else:
            lax.fori_loop(1, zs, from_x(y), 0)

    def c_copy(o):
        return rc(part.at[o * 2 + 1 - core], from_core.at[o], c_send.at[o], c_recv.at[o], sib)

    def share(t, c):
        j = lax.rem(t + 1 + (z * 2 * depth * 2) // CHUNK, chunks)
        cols = pl.ds(pl.multiple_of(j * CHUNK, CHUNK), CHUNK)
        r = dot(og[:, cols], attn[...], 0, 0).astype(BF16)
        part[pl.ds(j * per_chunk, per_chunk)] = r.reshape(per_chunk, depth, 2 * half)
        for b in range(per_chunk // 2):
            c_copy(j * (per_chunk // 2) + b).start()
        lax.fori_loop((t * zs) // chunks, ((t + 1) * zs) // chunks, from_y, 0)
        return c

    lax.fori_loop(0, chunks, share, 0)

    def y_copy(zz):
        return rc(y_out.at[zz], y_in.at[zz], y_send.at[zz], y_recv.at[zz], ypeer)

    def stage_y(step, c):
        zz = lax.rem(z + step, zs)
        o = zz * 2 + 1 - y
        c_copy(o).wait_recv()
        y_out[zz] = (part[o * 2 + core].astype(F32) + from_core[o].astype(F32)).astype(BF16)
        y_copy(zz).start()
        return c

    lax.fori_loop(1, zs + 1, stage_y, 0)

    def attn_grad(h):
        for part_of in range(half // CHUNK):
            cols = slice(part_of * CHUNK, (part_of + 1) * CHUNK)
            r = dot(og[...], wbuf[h, :, :, cols].reshape(n * depth, CHUNK), 1, 0)
            at = pl.ds(pl.multiple_of(h * half + part_of * CHUNK, CHUNK), CHUNK)
            da[:, at] = r.astype(BF16)

    def back_copy(i, part_of):
        src, dst = ((dk_out, dk_in), (dv_out, dv_in))[part_of]
        at = 2 * i + part_of
        return rc(src.at[i], dst.at[i], back_send.at[at], back_recv.at[at], down)

    def backward_half(i):
        def backward(j, c):
            keys, own = ext(k, k_halo, i, j)
            values, _ = ext(v, v_halo, i, j)
            at = pl.ds(pl.multiple_of(j * HD, HD), HD)
            d = da[:, own]
            probs = probs_buf[i * (H // 2) + j]
            delta = jnp.sum(d.astype(F32) * ctx_buf[:, own], axis=-1, keepdims=True)
            sg = (probs * (dot(d, values, 1, 1) - delta) * inv_scale).astype(BF16)
            dk = dot(sg, q[:, own], 0, 0)
            dv = dot(probs.astype(BF16), d, 0, 0)
            dk_out[i, :, at] = dk[:rows].astype(BF16)
            dv_out[i, :, at] = dv[:rows].astype(BF16)
            dk_own[:, own] = dk[rows:]
            dv_own[:, own] = dv[rows:]
            qg[:, own] = dot(sg, keys, 1, 0).astype(BF16)
            return c

        lax.fori_loop(0, H // 2, backward, 0)

        @pl.when(me > 0)
        def _():
            for part_of in range(2):
                back_copy(i, part_of).start()

    def z_copy(zz, slot):
        return rc(z_out.at[zz], z_in.at[slot], z_send.at[zz], z_recv.at[slot], (g, index(zz, y, core)))

    def summed(zz):
        o = zz * 2 + y
        c_copy(o).wait_recv()
        y_copy(zz).wait_recv()
        return part[o * 2 + core].astype(F32) + from_core[o].astype(F32) + y_in[zz].astype(F32)

    def stage_z(step, c):
        zz = lax.rem(z + step, zs)
        z_out[zz] = summed(zz).astype(BF16)
        z_copy(zz, z).start()
        return c

    early = 1 + zs // 2
    lax.fori_loop(0, n // 2, from_sib(hm), 0)
    attn_grad(hm)
    backward_half(hm)
    lax.fori_loop(1, early, stage_z, 0)
    lax.fori_loop(0, zs, from_x(1 - y), 0)
    lax.fori_loop(0, n // 2, from_sib(ho), 0)
    attn_grad(ho)
    backward_half(ho)
    lax.fori_loop(early, zs, stage_z, 0)

    def layer(j, c):
        rows_of = pl.ds(j * per_chunk, per_chunk)
        r = dot(attn[:, :half], wbuf[0, rows_of].reshape(CHUNK, half), 1, 1)
        r = r + dot(attn[:, half:], wbuf[1, rows_of].reshape(CHUNK, half), 1, 1)
        lo[:, pl.ds(pl.multiple_of(j * CHUNK, CHUNK), CHUNK)] = r.astype(BF16)
        return c

    lax.fori_loop(0, chunks, layer, 0)

    wg[...] = summed(z)

    for i in range(2):
        cols = slice(i * half, (i + 1) * half)

        @pl.when(me < n - 1)
        def _():
            for part_of in range(2):
                back_copy(i, part_of).wait_recv()
            kg[:, cols] = (dk_own[:, cols] + dk_in[i].astype(F32)).astype(BF16)
            vg[:, cols] = (dv_own[:, cols] + dv_in[i].astype(F32)).astype(BF16)

        @pl.when(me == n - 1)
        def _():
            kg[:, cols] = dk_own[:, cols].astype(BF16)
            vg[:, cols] = dv_own[:, cols].astype(BF16)

    def last(step, c):
        zz = lax.rem(z + step, zs)
        z_copy(zz, zz).wait_recv()
        wg[...] += z_in[zz].astype(F32)
        return c

    lax.fori_loop(1, zs, last, 0)

    @pl.when(me < n - 1)
    def _():
        for i in range(2):
            for part_of in range(2):
                halo(i, part_of).wait_send()

    @pl.when(me > 0)
    def _():
        for i in range(2):
            for part_of in range(2):
                back_copy(i, part_of).wait_send()

    def sent(step, c):
        zz = lax.rem(z + step, zs)
        mine = index(zz, y, core)
        other = index(zz, 1 - y, core)
        w_copy(0, hm, mine, ypeer).wait_send()
        w_copy(1, hm, other, xpeer).wait_send()
        w_copy(2, hm, mine, sib).wait_send()
        w_copy(2, ho, mine, sib).wait_send()
        w_copy(2, hm, other, sib).wait_send()
        w_copy(2, ho, other, sib).wait_send()
        y_copy(zz).wait_send()
        c_copy(zz * 2).wait_send()
        c_copy(zz * 2 + 1).wait_send()

        @pl.when(step > 0)
        def _():
            z_own(step).wait_send()
            w_copy(1, hm, mine, xpeer).wait_send()
            z_copy(zz, z).wait_send()

        return c

    lax.fori_loop(0, zs, sent, 0)


def per_device(n, queries, key_rows, value_rows, out_grad, out_weight, pair_allowed):
    rows, width = queries.shape
    model = out_grad.shape[1]
    depth = out_weight.shape[0]
    zs = n // 4
    half = width // 2
    vmem = pl.BlockSpec(memory_space=pltpu.VMEM)
    dma = pltpu.SemaphoreType.DMA
    return pl.pallas_call(
        functools.partial(kernel, n),
        out_shape=(
            jax.ShapeDtypeStruct((rows, model), BF16),
            jax.ShapeDtypeStruct((rows, width), BF16),
            jax.ShapeDtypeStruct((rows, width), BF16),
            jax.ShapeDtypeStruct((rows, width), BF16),
            jax.ShapeDtypeStruct((depth, width), F32),
        ),
        in_specs=[pl.BlockSpec(memory_space=pltpu.SMEM)] + [vmem] * 5,
        out_specs=(vmem,) * 5,
        scratch_shapes=[
            pltpu.VMEM((2, n, depth, half), BF16),
            pltpu.VMEM((n, depth, width), BF16),
            pltpu.VMEM((n // 2, depth, width), BF16),
            pltpu.VMEM((zs, depth, width), BF16),
            pltpu.VMEM((zs, depth, width), BF16),
            pltpu.VMEM((zs, depth, width), BF16),
            pltpu.VMEM((zs, depth, width), BF16),
        ]
        + [pltpu.VMEM((2, rows, half), BF16)] * 6
        + [
            pltpu.VMEM((rows, width), F32),
            pltpu.VMEM((rows, width), F32),
            pltpu.VMEM((H, rows, rows + SPAN * BLK), F32),
            pltpu.VMEM((rows, width), F32),
            pltpu.VMEM((rows, width), BF16),
            pltpu.VMEM((rows, width), BF16),
            pltpu.VMEM((rows, rows + SPAN * BLK), F32),
            dma((4, 2, n)),
            dma((2, n)),
            dma((4,)), dma((4,)), dma((4,)), dma((4,)),
            dma((n // 2,)), dma((n // 2,)),
            dma((zs,)), dma((zs,)), dma((zs,)), dma((zs,)),
        ],
        compiler_params=pltpu.CompilerParams(
            collective_id=0, has_side_effects=True, vmem_limit_bytes=52 * 2**20
        ),
    )(pair_allowed, queries, key_rows, value_rows, out_grad, out_weight)


def solution(mesh):
    both = P(("groups", "ctx"), None)
    return jax.shard_map(
        functools.partial(per_device, mesh.shape["ctx"]),
        mesh=mesh,
        in_specs=(both, both, both, both, P("ctx", None), P("groups", None)),
        out_specs=(both,) * 5,
        check_vma=False,
    )
```
